512 devices in a mesh: lon: 128 (over x_lo, y, z), lat: 4 (over x_hi, core).
Axes of the slice: x: 4 (x_hi: 2, x_lo: 2; x = x_hi * 2 + x_lo), y: 8, z: 8, core: 2. Of those that a mesh axis runs over, the one named last changes fastest.
Arguments:
- latent: bfloat16 [1, 48, 3072, 512], P(None, 'lat', 'lon'), may hold values from -6 to 6
- admit_mask: int32 [48, 3072], P('lat', 'lon'), may hold values 0 or 1
- fine_params: bfloat16 [1048576], P('lon')
- coarse_params: bfloat16 [6291456], P('lon')
Outputs:
- skip_tokens: bfloat16 [1, 48, 3072, 512], P(None, 'lat', 'lon')
- coarse_tokens: bfloat16 [1, 24, 1536, 1024], P(None, 'lat', 'lon')
The draws below stay inside these ranges and needn't reach their ends.
All inputs are finite; a program needn't handle non-finite values. No bound on the sum of `admit_mask` on one device may be relied on, other than what follows from the above.
Results may differ from the reference program's by a relative error of at most 0.015.
Values may be sent and summed in bfloat16 or wider, within the bound.
No kernel may reach another device: no remote copies, remote signals or barrier semaphores. Data moves between devices by JAX's collectives and lax.ppermute only.
A program may use at most 128 MiB of HBM per device.

```python
import math
import jax
import jax.numpy as jnp
from jax import lax

D = 512
FINE_HEADS = 8
COARSE_HEADS = 16
LEVELS = 1
WIN_LAT = 6
WIN_LON = 12
H = 48
W = 3072


def drawn_block(key, row_count, col_count, fan_in):
    return jax.random.normal(key, (row_count * col_count,), jnp.float32) / math.sqrt(fan_in)


def draw_fine_params(key, part):
    key = jax.random.fold_in(key, 7)
    key_one, key_two = jax.random.split(key)
    inputs = drawn_block(key_one, D, 3 * D, D)
    projection = drawn_block(key_two, D, D, D)
    return jnp.concatenate([inputs, projection]).astype(jnp.bfloat16)


def draw_coarse_params(key, part):
    key = jax.random.fold_in(key, 13)
    key_one, key_two, key_three = jax.random.split(key, 3)
    merging = drawn_block(key_one, 4 * D, 2 * D, 4 * D)
    inputs = drawn_block(key_two, 2 * D, 6 * D, 2 * D)
    projection = drawn_block(key_three, 2 * D, 2 * D, 2 * D)
    return jnp.concatenate([merging, inputs, projection]).astype(jnp.bfloat16)


def place_ends(drawn, own_key, smallest, high):
    longest = drawn.shape.index(max(drawn.shape))
    spots = []
    for shift in (0, 1):
        where = [jax.random.randint(jax.random.fold_in(own_key, axis), (), 0, length) for axis, length in enumerate(drawn.shape)]
        where[longest] = (where[longest] + shift) % drawn.shape[longest]
        spots.append(tuple(where))
    return drawn.at[spots[0]].set(smallest).at[spots[1]].set(high)


def shard_levels(stream_key, shape, cuts, least, top_value):
    def one(dim, shards_of):
        draws = jax.random.uniform(jax.random.fold_in(jax.random.fold_in(stream_key, 6), dim), (shards_of,), jnp.float32, least / len(cuts), top_value / len(cuts))
        return jnp.repeat(jnp.exp(draws), shape[dim] // shards_of).reshape((-1,) + (1,) * (len(shape) - dim - 1))

    gain = one(*cuts[0])
    for cut in cuts[1:]:
        gain = gain * one(*cut)
    return gain


def noise(key, shape, deviation, reach, cuts=(), kind=jnp.bfloat16):
    entries = deviation * jax.random.normal(key, shape, jnp.float32)
    if cuts:
        entries = entries * shard_levels(key, shape, cuts, -0.22, 0.18)
    return jnp.clip(entries, -reach, reach).astype(kind)


def setup_inputs(seed: int = 0) -> dict:
    keys = jax.random.split(jax.random.key(seed), 5)
    return {
        "latent": noise(keys[0], (LEVELS, H, W, D), 1.0, 6.0, ((1, 4), (2, 128))),
        "admit_mask": place_ends((jax.random.randint(keys[1], (H, W), 0, 4) < 3).astype(jnp.int32), jax.random.fold_in(keys[1], 1), 0, 1),
        "fine_params": draw_fine_params(jax.random.fold_in(keys[4], 71), 0),
        "coarse_params": draw_coarse_params(jax.random.fold_in(keys[4], 71), 0),
    }


epsilon = 1e-05

def layer_norm(values):
    values = values.astype(jnp.float32)
    centered = values - lax.optimization_barrier(jnp.mean(values, axis=-1, keepdims=True))
    spread = lax.optimization_barrier(jnp.mean(centered * centered, axis=-1, keepdims=True))
    return (centered * lax.rsqrt(spread + epsilon)).astype(jnp.bfloat16)

def project(values, matrix):
    return jnp.dot(values, matrix, preferred_element_type=jnp.float32).astype(jnp.bfloat16)

def attend(queries, key_values, admitted, head_count):
    levels, row_count, col_count, channels = queries.shape
    head_size = channels // head_count
    win_rows = row_count // WIN_LAT
    win_cols = col_count // WIN_LON
    window_len = levels * WIN_LAT * WIN_LON

    def windows(values, segments):
        arranged = values.reshape(levels, win_rows, WIN_LAT, win_cols, WIN_LON, segments, head_count, head_size)
        arranged = arranged.transpose(1, 3, 5, 6, 0, 2, 4, 7)
        return arranged.reshape(win_rows, win_cols, segments, head_count, window_len, head_size)
    query_win = windows(queries, 1)[:, :, 0].astype(jnp.float32)
    both = windows(key_values, 2).astype(jnp.float32)
    key_win = both[:, :, 0]
    value_win = both[:, :, 1]
    key_mask = admitted.reshape(win_rows, WIN_LAT, win_cols, WIN_LON).transpose(0, 2, 1, 3)
    key_mask = jnp.broadcast_to(key_mask[:, :, None], (win_rows, win_cols, levels, WIN_LAT, WIN_LON))
    key_mask = key_mask.reshape(win_rows, win_cols, 1, 1, window_len)
    allowed = (key_mask > 0) | jnp.eye(window_len, dtype=bool)
    scores = jnp.einsum('abhqd,abhkd->abhqk', query_win, key_win) / math.sqrt(head_size)
    scores = jnp.where(allowed, scores, -jnp.inf)
    highest = lax.optimization_barrier(jnp.max(scores, axis=-1, keepdims=True))
    raised = jnp.exp(scores - highest)
    attention = (raised / lax.optimization_barrier(jnp.sum(raised, axis=-1, keepdims=True))).astype(jnp.bfloat16)
    blended = jnp.einsum('abhqk,abhkd->abhqd', attention.astype(jnp.float32), value_win).astype(jnp.bfloat16)
    blended = blended.reshape(win_rows, win_cols, head_count, levels, WIN_LAT, WIN_LON, head_size)
    blended = blended.transpose(3, 0, 4, 1, 5, 2, 6)
    return blended.reshape(levels, row_count, col_count, channels)

def reference(latent, admit_mask, fine_params, coarse_params):
    channels = D
    square = channels * channels
    fine_inputs = fine_params[:3 * square].reshape(channels, 3 * channels)
    fine_output = fine_params[3 * square:].reshape(channels, channels)
    coarse_merge = coarse_params[:8 * square].reshape(4 * channels, 2 * channels)
    coarse_inputs = coarse_params[8 * square:20 * square].reshape(2 * channels, 6 * channels)
    coarse_output = coarse_params[20 * square:].reshape(2 * channels, 2 * channels)
    rim_lat = WIN_LAT // 2
    rim_lon = WIN_LON // 2
    rolled = jnp.roll(latent, rim_lon, axis=2)
    admitted = jnp.roll(admit_mask, rim_lon, axis=1).astype(jnp.float32)
    columns = W // WIN_LON
    fine_blocks = rolled.reshape(LEVELS, H, columns, WIN_LON, channels).transpose(2, 0, 1, 3, 4)
    fine_masks = admitted.reshape(H, columns, WIN_LON).transpose(1, 0, 2)

    def fine_column(items):
        column, key_mask = items
        normed = layer_norm(column)
        queries = project(normed, fine_inputs[:, :channels])
        key_values = project(normed, fine_inputs[:, channels:])
        padding = ((0, 0), (rim_lat, rim_lat), (0, 0), (0, 0))
        blended = attend(jnp.pad(queries, padding), jnp.pad(key_values, padding), jnp.pad(key_mask, ((rim_lat, rim_lat), (0, 0))), FINE_HEADS)
        blended = blended[:, rim_lat:rim_lat + H]
        return (column + jnp.dot(blended, fine_output, preferred_element_type=jnp.float32)).astype(jnp.bfloat16)
    results = lax.map(fine_column, (fine_blocks, fine_masks))
    skip_tokens = results.transpose(1, 2, 0, 3, 4).reshape(LEVELS, H, W, channels)
    skip_tokens = jnp.roll(skip_tokens, -rim_lon, axis=2)
    half_rows = H // 2
    groups = W // (2 * WIN_LON)
    coarse_blocks = skip_tokens.reshape(LEVELS, H, groups, 2 * WIN_LON, channels).transpose(2, 0, 1, 3, 4)
    coarse_admit = admit_mask.reshape(half_rows, 2, W // 2, 2).max(axis=(1, 3)).astype(jnp.float32)
    coarse_masks = coarse_admit.reshape(half_rows, groups, WIN_LON).transpose(1, 0, 2)

    def coarse_column(items):
        column, key_mask = items
        stacked = column.reshape(LEVELS, half_rows, 2, WIN_LON, 2, channels).transpose(0, 1, 3, 4, 2, 5)
        stacked = stacked.reshape(LEVELS, half_rows, WIN_LON, 4 * channels)
        merged = project(layer_norm(stacked), coarse_merge)
        coarse_normed = layer_norm(merged)
        coarse_queries = project(coarse_normed, coarse_inputs[:, :2 * channels])
        coarse_pairs = project(coarse_normed, coarse_inputs[:, 2 * channels:])
        blended = attend(coarse_queries, coarse_pairs, key_mask, COARSE_HEADS)
        return (merged + jnp.dot(blended, coarse_output, preferred_element_type=jnp.float32)).astype(jnp.bfloat16)
    coarse_results = lax.map(coarse_column, (coarse_blocks, coarse_masks))
    coarse_tokens = coarse_results.transpose(1, 2, 0, 3, 4).reshape(LEVELS, half_rows, W // 2, 2 * channels)
    return (skip_tokens, coarse_tokens)
```

```python
import math

import jax
import jax.numpy as jnp
from jax import lax
from jax.sharding import Mesh
from jax.sharding import PartitionSpec as P

FINE_HEADS = 8
COARSE_HEADS = 16
WIN_LAT = 6
WIN_LON = 12


epsilon = 1e-05
LON = ("xl", "y", "z")
LAT = ("xh", "c")


def with_halo(cells, sides, width, closed):
    for axis, dim in sides:
        count = lax.axis_size(axis)
        ends = count if closed else count - 1
        head = lax.slice_in_dim(cells, 0, width, axis=dim)
        tail = lax.slice_in_dim(cells, cells.shape[dim] - width, cells.shape[dim], axis=dim)
        cells = jnp.concatenate(
            [
                lax.ppermute(tail, axis, [(i, (i + 1) % count) for i in range(ends)]),
                cells,
                lax.ppermute(head, axis, [((i + 1) % count, i) for i in range(ends)]),
            ],
            axis=dim,
        )
    return cells


def layer_norm(values):
    values = values.astype(jnp.float32)
    centered = values - jnp.mean(values, axis=-1, keepdims=True)
    spread = jnp.mean(centered * centered, axis=-1, keepdims=True)
    return (centered * lax.rsqrt(spread + epsilon)).astype(jnp.bfloat16)


def project(values, matrix):
    return jnp.dot(values, matrix, preferred_element_type=jnp.float32).astype(jnp.bfloat16)


def attend(queries, key_values, admitted, head_count):
    levels, row_count, col_count, channels = queries.shape
    head_size = channels // head_count
    win_rows = row_count // WIN_LAT
    win_cols = col_count // WIN_LON
    window_len = levels * WIN_LAT * WIN_LON

    def windows(values, segments):
        arranged = values.reshape(
            levels, win_rows, WIN_LAT, win_cols, WIN_LON, segments, head_count, head_size
        )
        arranged = arranged.transpose(1, 3, 5, 6, 0, 2, 4, 7)
        return arranged.reshape(win_rows, win_cols, segments, head_count, window_len, head_size)

    query_win = windows(queries, 1)[:, :, 0]
    both = windows(key_values, 2)
    key_mask = admitted.reshape(win_rows, WIN_LAT, win_cols, WIN_LON).transpose(0, 2, 1, 3)
    key_mask = key_mask[:, :, None]
    key_mask = key_mask.reshape(win_rows, win_cols, window_len)
    diagonal = jnp.eye(window_len, dtype=bool)

    def one_row(items):
        row_queries, row_pairs, row_mask = items
        scores = jnp.einsum(
            "bhqd,bhkd->bhqk", row_queries, row_pairs[:, 0], preferred_element_type=jnp.float32
        ) / math.sqrt(head_size)
        allowed = (row_mask[:, None, None, :] > 0) | diagonal
        scores = jnp.where(allowed, scores, -jnp.inf)
        highest = jnp.max(scores, axis=-1, keepdims=True)
        raised = jnp.exp(scores - highest)
        attention = (raised / jnp.sum(raised, axis=-1, keepdims=True)).astype(jnp.bfloat16)
        return jnp.einsum(
            "bhqk,bhkd->bhqd", attention, row_pairs[:, 1], preferred_element_type=jnp.float32
        ).astype(jnp.bfloat16)

    blended = lax.map(one_row, (query_win, both, key_mask))
    blended = blended.reshape(win_rows, win_cols, head_count, levels, WIN_LAT, WIN_LON, head_size)
    blended = blended.transpose(3, 0, 4, 1, 5, 2, 6)
    return blended.reshape(levels, row_count, col_count, channels)


def gather_params(fine_params, coarse_params):
    fine_count = fine_params.shape[0]
    width = 1024
    packed = jnp.concatenate([fine_params, coarse_params]).reshape(-1, width)
    pair = lax.all_gather(packed, "xl", axis=0, tiled=False)
    every = lax.all_gather(pair, ("y", "z"), axis=0, tiled=False)
    every = every.transpose(1, 0, 2, 3).reshape(-1, *packed.shape)
    fine_rows = fine_count // width
    return every[:, :fine_rows].reshape(-1), every[:, fine_rows:].reshape(-1)


def local(latent, admit_mask, fine_params, coarse_params):
    channels = latent.shape[-1]
    levels = latent.shape[0]
    square = channels * channels
    lat_rows, lon_cols = admit_mask.shape
    rim_lat = WIN_LAT // 2
    rim_lon = WIN_LON // 2
    fine_flat, coarse_flat = gather_params(fine_params, coarse_params)
    fine_inputs = fine_flat[: 3 * square].reshape(channels, 3 * channels)
    fine_output = fine_flat[3 * square :].reshape(channels, channels)
    normed = layer_norm(latent)
    queries = project(normed, fine_inputs[:, :channels])
    outgoing = project(normed, fine_inputs[:, channels:])
    admitted = admit_mask.astype(jnp.bfloat16)[None]
    outgoing, admitted = (
        with_halo(outgoing, ((LAT, 1),), rim_lat, False),
        with_halo(admitted, ((LAT, 1),), rim_lat, False),
    )
    outgoing, admitted = (
        with_halo(outgoing, ((LON, 2),), rim_lon, True),
        with_halo(admitted, ((LON, 2),), rim_lon, True),
    )
    padding = ((0, 0), (rim_lat, rim_lat), (rim_lon, rim_lon), (0, 0))
    blended = attend(
        jnp.pad(queries, padding), outgoing, admitted[0].astype(jnp.float32), FINE_HEADS
    )
    blended = blended[:, rim_lat : rim_lat + lat_rows, rim_lon : rim_lon + lon_cols]
    skip_tokens = (
        latent + jnp.dot(blended, fine_output, preferred_element_type=jnp.float32)
    ).astype(jnp.bfloat16)
    coarse_merge = coarse_flat[: 8 * square].reshape(4 * channels, 2 * channels)
    coarse_inputs = coarse_flat[8 * square : 20 * square].reshape(2 * channels, 6 * channels)
    coarse_output = coarse_flat[20 * square :].reshape(2 * channels, 2 * channels)
    stacked = skip_tokens.reshape(levels, lat_rows // 2, 2, lon_cols // 2, 2, channels).transpose(
        0, 1, 3, 4, 2, 5
    )
    stacked = stacked.reshape(levels, lat_rows // 2, lon_cols // 2, 4 * channels)
    merged = project(layer_norm(stacked), coarse_merge)
    coarse_normed = layer_norm(merged)
    coarse_queries = project(coarse_normed, coarse_inputs[:, : 2 * channels])
    coarse_pairs = project(coarse_normed, coarse_inputs[:, 2 * channels :])
    coarse_admit = (
        admit_mask.reshape(lat_rows // 2, 2, lon_cols // 2, 2).max(axis=(1, 3)).astype(jnp.float32)
    )
    coarse_mixed = attend(coarse_queries, coarse_pairs, coarse_admit, COARSE_HEADS)
    coarse_tokens = (
        merged + jnp.dot(coarse_mixed, coarse_output, preferred_element_type=jnp.float32)
    ).astype(jnp.bfloat16)
    return (skip_tokens, coarse_tokens)


def solution(mesh):
    split = Mesh(mesh.devices.reshape(2, 8, 8, 2, 2), (*LON, *LAT))
    return jax.shard_map(
        local,
        mesh=split,
        in_specs=(P(None, LAT, LON, None), P(LAT, LON), P(LON), P(LON)),
        out_specs=(P(None, LAT, LON, None), P(None, LAT, LON, None)),
        check_vma=False,
    )
```

```python
import math

import jax
import jax.numpy as jnp
import numpy as np
from jax import lax
from jax.experimental import pallas as pl
from jax.experimental.pallas import tpu as pltpu
from jax.sharding import Mesh
from jax.sharding import PartitionSpec as P

FINE_HEADS = 8
COARSE_HEADS = 16
HEAD = 64
WIN_LAT = 6
WIN_LON = 12
LON = ("xl", "y", "z")
LAT = ("xh", "c")

epsilon = 1e-05

ROWS, COLS = 12, 24
WIN = WIN_LAT * WIN_LON
WIN_PAD = 80
CELL_PAD = 16
COARSE_PAD = WIN_LAT * CELL_PAD
CELLS = 4 * COARSE_PAD
GROUP = 4


def token_orders():
    top, side = WIN_LAT // 2, WIN_LON // 2
    own = ROWS * COLS
    high = ROWS + 2 * top

    def source(row, col):
        if col < side:
            return own + 2 * top * COLS + row * side + col
        if col >= side + COLS:
            return own + 2 * top * COLS + high * side + row * side + col - side - COLS
        col -= side
        if row < top:
            return own + row * COLS + col
        if row >= top + ROWS:
            return own + top * COLS + (row - top - ROWS) * COLS + col
        return (row - top) * COLS + col

    windows, counts, place = [], [], {}
    for a in range(high // WIN_LAT):
        for b in range((COLS + 2 * side) // WIN_LON):
            inner, outer = [], []
            for row in range(a * WIN_LAT, (a + 1) * WIN_LAT):
                for col in range(b * WIN_LON, (b + 1) * WIN_LON):
                    at = source(row, col)
                    (inner if at < own else outer).append(at)
            for k, at in enumerate(inner):
                place[at] = (len(counts), k)
            counts.append(-(-len(inner) // 16) * 16)
            windows.append(inner + outer + [-1] * (WIN_PAD - WIN))
    starts = np.concatenate([[0], np.cumsum(counts)])
    blended_at = {at: starts[w] + k for at, (w, k) in place.items()}
    cells = -np.ones((2, 2, WIN_LAT, CELL_PAD), np.int32)
    for row in range(ROWS):
        for col in range(COLS):
            cells[col % 2, row % 2, row // 2, col // 2] = row * COLS + col
    cells = cells.reshape(-1)
    from_blended = np.array([blended_at[c] if c >= 0 else -1 for c in cells], np.int32)
    back = np.zeros(own, np.int32)
    for k, c in enumerate(cells):
        if c >= 0:
            back[c] = k
    return np.array(windows, np.int32).reshape(-1), counts, cells, from_blended, back


WINDOWS, COUNTS, CELL_OF, FROM_BLENDED, BACK = token_orders()
SOURCES = ROWS * COLS + WIN_LAT * COLS + WIN_LON * (ROWS + WIN_LAT)


def one_hot(index, width):
    return (jnp.asarray(index)[:, None] == jnp.arange(width, dtype=jnp.int32)).astype(jnp.bfloat16)


def layer_norm(values):
    values = values.astype(jnp.float32)
    centered = values - jnp.mean(values, axis=-1, keepdims=True)
    spread = jnp.mean(centered * centered, axis=-1, keepdims=True)
    return (centered * lax.rsqrt(spread + epsilon)).astype(jnp.bfloat16)


def dot(left, right):
    return jnp.dot(left, right, preferred_element_type=jnp.float32)


def attend(queries, keys, values, bias):
    count = queries.shape[0]
    lane = lax.broadcasted_iota(jnp.int32, (1, GROUP * HEAD), 1) // HEAD
    spread = jnp.concatenate(
        [jnp.where(lane == h, queries, jnp.zeros_like(queries)) for h in range(GROUP)], axis=0
    )
    scores = lax.dot_general(
        spread, keys, (((1,), (1,)), ((), ())), preferred_element_type=jnp.float32
    )
    scores = scores * (1.0 / math.sqrt(HEAD)) + jnp.concatenate([bias] * GROUP, axis=0)
    raised = jnp.exp(scores - jnp.max(scores, axis=-1, keepdims=True))
    total = jnp.sum(raised, axis=-1, keepdims=True)
    mixed = dot(raised.astype(jnp.bfloat16), values) * (1.0 / total)
    out = jnp.where(lane == 0, mixed[:count], 0.0)
    for h in range(1, GROUP):
        out = jnp.where(lane == h, mixed[h * count : (h + 1) * count], out)
    return out.astype(jnp.bfloat16)


def fine_block(
    tokens, bias, cells, from_blended, back, weights, wide, queries, key_values, blended, skip, arrived
):
    channels = tokens.shape[1]
    width, lane = channels // 2, 128
    blocks = width // lane
    own = jnp.concatenate(
        [tokens[w * WIN_PAD : w * WIN_PAD + n] for w, n in enumerate(COUNTS)], axis=0
    )
    sides = []
    for c in range(2):
        arrived(c)
        side = weights[c].reshape(-1, width)
        sides.append(side)
        for b in range(blocks):
            wide[c * blocks + b] = side[: 3 * channels, b * lane : (b + 1) * lane].astype(
                jnp.float32
            )
        lanes = slice(c * width, (c + 1) * width)
        for j in range(3):
            matrix = jnp.concatenate(
                [
                    wide[c * blocks + b, pl.ds(j, channels, stride=3), :].astype(jnp.bfloat16)
                    for b in range(blocks)
                ],
                axis=1,
            )
            if j:
                key_values[j - 1, :, lanes] = dot(tokens[...], matrix).astype(jnp.bfloat16)
            else:
                queries[:, lanes] = dot(own, matrix).astype(jnp.bfloat16)
    start = 0
    span = GROUP * HEAD
    for w, count in enumerate(COUNTS):
        at = w * WIN_PAD
        for g in range(channels // span):
            lanes = slice(g * span, (g + 1) * span)
            blended[start : start + count, lanes] = attend(
                queries[start : start + count, lanes],
                key_values[0, at : at + WIN_PAD, lanes],
                key_values[1, at : at + WIN_PAD, lanes],
                bias[w, :count, :],
            )
        start += count
    ordered = dot(from_blended[...], blended[...]).astype(jnp.bfloat16)
    added = jnp.concatenate([dot(ordered, side[3 * channels :]) for side in sides], axis=1)
    tokens_out = (cells[...].astype(jnp.float32) + added).astype(jnp.bfloat16)
    skip[...] = dot(back[...], tokens_out).astype(jnp.bfloat16)
    joined = jnp.concatenate(
        [tokens_out[k * COARSE_PAD : (k + 1) * COARSE_PAD] for k in range(4)], axis=1
    )
    return layer_norm(joined)


def kernel(
    core,
    tokens,
    bias,
    cells,
    from_blended,
    back,
    coarse_bias,
    mine,
    other,
    skip,
    out,
    fine_weights,
    wide,
    queries,
    key_values,
    fine_blended,
    weights,
    spread,
    qkv,
    blended,
    fine_arrived,
    arrived,
):
    cores, pairs, ys, zs, fine_rows, block_width = fine_weights.shape
    blocks, rows = weights.shape[0], weights.shape[4]
    parts = blocks // cores
    channels = 2 * tokens.shape[1]

    def fine_copies(side, held):
        here = pl.ds(parts * rows, fine_rows)
        found = []
        for pair in range(pairs):
            for k in range(1 if side == 0 else zs):
                source = held.at[:, :, pair, here] if side == 0 else held.at[k, :, pair, here]
                target = fine_weights.at[side, pair]
                target = target if side == 0 else target.at[:, k]
                found.append(pltpu.make_async_copy(source, target, fine_arrived.at[side, pair, k]))
        return found

    def coarse_copies(side, held, pair):
        found = []
        for part in range(parts):
            here = pl.ds(part * rows, rows)
            for k in range(1 if side == 0 else zs):
                source = held.at[:, :, pair, here] if side == 0 else held.at[k, :, pair, here]
                target = weights.at[side * parts + part, pair]
                target = target if side == 0 else target.at[:, k]
                found.append(
                    pltpu.make_async_copy(source, target, arrived.at[side, pair, part, k])
                )
        return found

    def begin(start):
        @pl.when(core[0] == 0)
        def _():
            start((mine, other))

        @pl.when(core[0] != 0)
        def _():
            start((other, mine))

    def start_fine(held):
        for side in range(cores):
            for copy in fine_copies(side, held[side]):
                copy.start()

    def start_coarse(held):
        for pair in range(pairs):
            for side in range(cores):
                for copy in coarse_copies(side, held[side], pair):
                    copy.start(priority=1)

    def fine_wait(side):
        for copy in fine_copies(side, mine):
            copy.wait()
        if side == 0:
            begin(start_coarse)

    def wait(pair):
        for side in range(cores):
            for copy in coarse_copies(side, mine, pair):
                copy.wait()

    begin(start_fine)

    def times(left, first, last):
        sums = []
        for q in range(blocks):
            sums.append(dot(left, weights[q].reshape(-1, block_width)[first:last]))
        return jnp.concatenate(sums, axis=1)

    joined = fine_block(
        tokens,
        bias,
        cells,
        from_blended,
        back,
        fine_weights,
        wide,
        queries,
        key_values,
        fine_blended,
        skip,
        fine_wait,
    )
    merge_rows = 2 * channels
    wait(0)
    merged = times(joined, 0, merge_rows).astype(jnp.bfloat16)
    normed = layer_norm(merged)
    block = 128
    into = lax.broadcasted_iota(jnp.int32, (block, 9 * block), 1)
    places = (into // (3 * block)) + 3 * lax.broadcasted_iota(jnp.int32, (block, 9 * block), 0)
    places = (into % (3 * block) == places).astype(jnp.bfloat16)
    for b in range(channels // block):
        apart = dot(normed[:, b * block : (b + 1) * block], places).astype(jnp.bfloat16)
        for j in range(3):
            spread[j * COARSE_PAD : (j + 1) * COARSE_PAD, 3 * block * b : 3 * block * (b + 1)] = (
                apart[:, 3 * block * j : 3 * block * (j + 1)]
            )
    wait(1)
    qkv[...] = times(spread[...], merge_rows, merge_rows + 3 * channels).astype(jnp.bfloat16)
    span = GROUP * HEAD
    for g in range(channels // span):
        lanes = slice(g * span, (g + 1) * span)
        blended[:, lanes] = attend(
            qkv[:COARSE_PAD, lanes],
            qkv[COARSE_PAD : 2 * COARSE_PAD, lanes],
            qkv[2 * COARSE_PAD :, lanes],
            coarse_bias[...],
        )
    added = times(blended[...], merge_rows + 3 * channels, merge_rows + 4 * channels)
    result = (merged.astype(jnp.float32) + added).astype(jnp.bfloat16)
    out[...] = result.reshape(WIN_LAT, CELL_PAD, channels)[:, :WIN_LON]


VMEM = pl.BlockSpec(memory_space=pltpu.VMEM)


def run(core, tokens, bias, cells, coarse_bias, mine, other, fine_rows):
    outer, inner, pairs, packed_rows, block_width = mine.shape
    channels = tokens.shape[1]
    wider = 2 * channels
    cores, blocks = 2, wider // block_width
    rows = (packed_rows - fine_rows) * cores // blocks
    ys, zs = lax.axis_size("y"), lax.axis_size("z")
    hbm = pl.BlockSpec(memory_space=pltpu.HBM)
    return pl.pallas_call(
        kernel,
        out_shape=(
            jax.ShapeDtypeStruct((ROWS * COLS, channels), jnp.bfloat16),
            jax.ShapeDtypeStruct((WIN_LAT, WIN_LON, wider), jnp.bfloat16),
        ),
        in_specs=[pl.BlockSpec(memory_space=pltpu.SMEM)] + [VMEM] * 6 + [hbm] * 2,
        out_specs=(VMEM, VMEM),
        scratch_shapes=[
            pltpu.VMEM((cores, pairs, ys, zs, fine_rows, block_width), jnp.bfloat16),
            pltpu.VMEM((channels // 128, 3 * channels, 128), jnp.float32),
            pltpu.VMEM((sum(COUNTS), channels), jnp.bfloat16),
            pltpu.VMEM((2, tokens.shape[0], channels), jnp.bfloat16),
            pltpu.VMEM((sum(COUNTS), channels), jnp.bfloat16),
            pltpu.VMEM((blocks, pairs, ys, zs, rows, block_width), jnp.bfloat16),
            pltpu.VMEM((3 * COARSE_PAD, 3 * wider), jnp.bfloat16),
            pltpu.VMEM((3 * COARSE_PAD, wider), jnp.bfloat16),
            pltpu.VMEM((COARSE_PAD, wider), jnp.bfloat16),
            pltpu.SemaphoreType.DMA((cores, pairs, zs)),
            pltpu.SemaphoreType.DMA((cores, pairs, blocks // cores, zs)),
        ],
        compiler_params=pltpu.CompilerParams(vmem_limit_bytes=48 * 2**20),
        cost_estimate=pl.CostEstimate(
            flops=4 * 10**9, bytes_accessed=18 * 10**6, transcendentals=2 * 10**6
        ),
    )(
        core,
        tokens,
        bias,
        cells,
        one_hot(FROM_BLENDED, sum(COUNTS)),
        one_hot(BACK, CELLS),
        coarse_bias,
        mine,
        other,
    )


def neighbours(values, axes, dim, width, closed):
    count = lax.axis_size(axes)
    ends = count if closed else count - 1
    head = lax.slice_in_dim(values, 0, width, axis=dim)
    tail = lax.slice_in_dim(values, values.shape[dim] - width, values.shape[dim], axis=dim)
    before = lax.ppermute(tail, axes, [(i, (i + 1) % count) for i in range(ends)])
    after = lax.ppermute(head, axes, [((i + 1) % count, i) for i in range(ends)])
    return before, after


def gather_params(fine_params, coarse_params, channels):
    first = lax.axis_index("c") == 0
    quarter = channels // 2
    coarse = coarse_params.reshape(-1, 2 * channels)
    fine = fine_params.reshape(-1, channels)

    def columns(at):
        return [
            coarse[:, 2 * at * quarter : (2 * at + 1) * quarter],
            coarse[:, (2 * at + 1) * quarter : (2 * at + 2) * quarter],
            fine[:, at * quarter : (at + 1) * quarter],
        ]

    packed = jnp.where(
        first, jnp.concatenate(columns(0), axis=0), jnp.concatenate(columns(1), axis=0)
    )
    pair = lax.all_gather(packed, "xl", axis=0, tiled=False)
    ys, zs = lax.axis_size("y"), lax.axis_size("z")
    at = np.arange(2 * ys * zs).reshape(ys, zs, 2)
    along_y, along_z = [
        [at[:, z, c].tolist() for z in range(zs)] for c in range(2)
    ], [[at[y, :, c].tolist() for y in range(ys)] for c in range(2)]
    axes = ("y", "z", "c")
    held = lax.all_gather(pair, axes, axis_index_groups=along_z[0] + along_y[1])
    mine = lax.all_gather(held, axes, axis_index_groups=along_y[0] + along_z[1])
    return mine, fine.shape[0]


def local(latent, admit_mask, fine_params, coarse_params):
    channels = latent.shape[-1]
    mine, fine_rows = gather_params(fine_params, coarse_params, channels)

    extra = 128
    admitted = jnp.broadcast_to(
        admit_mask.astype(jnp.bfloat16)[:, :, None], (*admit_mask.shape, extra)
    )
    cells = jnp.concatenate([latent[0], admitted], axis=2)
    north, south = neighbours(cells, LAT, 0, WIN_LAT // 2, False)
    tall = jnp.concatenate([north, cells, south], axis=0)
    west, east = neighbours(tall, LON, 1, WIN_LON // 2, True)
    sources = jnp.concatenate(
        [v.reshape(-1, channels + extra) for v in (cells, north, south, west, east)], axis=0
    )
    placed = dot(one_hot(WINDOWS, SOURCES), sources)
    tokens = layer_norm(placed[:, :channels])
    fine_admit = placed[:, channels].reshape(-1, WIN_PAD)
    diagonal = jnp.eye(WIN_PAD, dtype=bool)
    fine_bias = jnp.where((fine_admit[:, None, :] > 0) | diagonal, 0.0, -jnp.inf)
    own = dot(one_hot(CELL_OF, ROWS * COLS), latent.reshape(-1, channels)).astype(jnp.bfloat16)

    coarse_admit = admit_mask.reshape(ROWS // 2, 2, COLS // 2, 2).max(axis=(1, 3))
    coarse_admit = jnp.pad(coarse_admit, ((0, 0), (0, CELL_PAD - COLS // 2))).reshape(1, -1)
    coarse_bias = jnp.where((coarse_admit > 0) | jnp.eye(COARSE_PAD, dtype=bool), 0.0, -jnp.inf)
    mine, tokens, fine_bias, own, coarse_bias = lax.optimization_barrier(
        (mine, tokens, fine_bias, own, coarse_bias)
    )
    other = lax.ppermute(mine, "c", [(0, 1), (1, 0)])
    core = lax.axis_index("c").reshape(1)
    skip, coarse = run(core, tokens, fine_bias, own, coarse_bias, mine, other, fine_rows)
    return skip.reshape(latent.shape), coarse[None]


def solution(mesh):
    split = Mesh(mesh.devices.reshape(2, 8, 8, 2, 2), (*LON, *LAT))
    return jax.shard_map(
        local,
        mesh=split,
        in_specs=(P(None, LAT, LON, None), P(LAT, LON), P(LON), P(LON)),
        out_specs=(P(None, LAT, LON, None), P(None, LAT, LON, None)),
        check_vma=False,
    )
```
